32 devices in a mesh: dp: 16 (over z, y, core), expert: 2 (over x).
Axes of the slice: x: 2, y: 2, z: 4, core: 2. Of those that a mesh axis runs over, the one named last changes fastest.
Arguments:
- tokens: bfloat16 [6144, 2048], P(('dp', 'expert')), may hold values from -6 to 6
- routes: int32 [6144, 6], P(('dp', 'expert')), may hold values from 0 to 63, as said below
- gate_scale: float32 [6144, 6], P(('dp', 'expert')), may hold values from 0.2 to 2
- w_gate: bfloat16 [2, 2048, 768], P('expert', 'dp'), may hold values from -0.125 to 0.125
- w_up: bfloat16 [2, 2048, 768], P('expert', 'dp'), may hold values from -0.125 to 0.125
- w_down: bfloat16 [2, 2048, 768], P('expert', 'dp'), may hold values from -0.21875 to 0.21875
- d_out: bfloat16 [6144, 2048], P(('dp', 'expert')), may hold values from -6 to 6
Outputs:
- layer_out: bfloat16 [6144, 2048], P(('dp', 'expert'))
- d_tokens: bfloat16 [6144, 2048], P(('dp', 'expert'))
- grad_gate: float32 [2, 2048, 768], P('expert', 'dp')
- grad_up: float32 [2, 2048, 768], P('expert', 'dp')
- grad_down: float32 [2, 2048, 768], P('expert', 'dp')
The draws below stay inside these ranges and needn't reach their ends.
Inputs may be any that keep to these rules, and one draw needn't show every extreme that they name: `routes`: each token names 6 different experts. The experts of this window are 0 to 1; among the 192 tokens of one device no window expert is named by more than 32 tokens.
All inputs are finite; a program needn't handle non-finite values.
Results may differ from the reference program's by a relative error of at most 0.02.
Values may be sent and summed in bfloat16 or wider, within the bound.
No kernel may reach another device: no remote copies, remote signals or barrier semaphores. Data moves between devices by JAX's collectives and lax.ppermute only.
A program may use at most 64 MiB of HBM per device.

```python
import math
import jax
import jax.numpy as jnp
from jax import lax

D = 2048
EXPERTS = 64
TOP = 6
H = 768
TOK_DEV = 192
CAP = 32
WINDOW = 2
TOKENS = 6144


def draw_routes(key, part):
    blocks = TOKENS // TOK_DEV
    stride = TOK_DEV // WINDOW
    others_count = EXPERTS - WINDOW
    k_count, k_rank, k_other, k_order = jax.random.split(key, 4)
    lower = (CAP + 3) // 4
    counts = jax.random.randint(k_count, (blocks, WINDOW), lower, CAP + 1)
    full_expert = jnp.arange(blocks) // WINDOW % WINDOW
    counts = jnp.where(jnp.arange(WINDOW)[None, :] == full_expert[:, None], CAP, counts)
    scores = jax.random.randint(k_rank, (blocks, TOK_DEV), 0, 2 ** 20) * TOK_DEV + jnp.arange(TOK_DEV)[None, :]
    order = jnp.argsort(scores, axis=1)
    rank = jnp.argsort(order, axis=1)
    offset = (rank[:, :, None] - stride * jnp.arange(WINDOW)[None, None, :]) % TOK_DEV
    member = offset < counts[:, None, :]
    number = jnp.sum(member.astype(jnp.int32), axis=2)
    window_key = jnp.where(member, jnp.arange(WINDOW)[None, None, :], WINDOW + jnp.arange(WINDOW)[None, None, :])
    window_sorted = jnp.sort(window_key, axis=2)
    other_scores = jax.random.randint(k_other, (blocks, TOK_DEV, others_count), 0, 2 ** 20) * others_count + jnp.arange(others_count)[None, None, :]
    other_ids = WINDOW + jnp.argsort(other_scores, axis=2)[:, :, :TOP]
    slot = jnp.broadcast_to(jnp.arange(TOP)[None, None, :], (blocks, TOK_DEV, TOP))
    pick_window = jnp.take_along_axis(window_sorted, jnp.minimum(slot, WINDOW - 1), axis=2)
    pick_other = jnp.take_along_axis(other_ids, jnp.clip(slot - number[:, :, None], 0, TOP - 1), axis=2)
    ids = jnp.where(slot < number[:, :, None], pick_window, pick_other)
    column_scores = jax.random.randint(k_order, (blocks, TOK_DEV, TOP), 0, 2 ** 20) * TOP + slot
    ids = jnp.take_along_axis(ids, jnp.argsort(column_scores, axis=2), axis=2)
    return ids.reshape(TOKENS, TOP).astype(jnp.int32)


def raised(result, stream_key, source, target, blocks, factor):
    def block_of(dim):
        return (jnp.arange(result.shape[dim]) // (result.shape[dim] // blocks)).reshape((-1,) + (1,) * (result.ndim - 1 - dim))

    one_side = jax.random.permutation(stream_key, blocks)[block_of(target)]
    other_side = (block_of(target) + blocks // 2) % blocks
    return jnp.where((block_of(source) == one_side) | (block_of(source) == other_side), factor * result, result)


def levels(key, extent, cuts, low, high):
    loudness, own = 1.0, jax.random.fold_in(key, 6)
    for dim, blocks in cuts:
        draws = jnp.exp(jax.random.uniform(jax.random.fold_in(own, dim), (blocks,), jnp.float32, low / len(cuts), high / len(cuts)))
        loudness = loudness * jnp.repeat(draws, extent[dim] // blocks).reshape([-1 if axis == dim else 1 for axis in range(len(extent))])
    return loudness


def normal_values(rng, shape, scale, limit, cuts=(), held_as=jnp.bfloat16):
    loudness = levels(rng, shape, cuts, -0.22, 0.18) if cuts else 1.0
    result = jax.random.normal(rng, shape, jnp.float32) * scale * loudness
    return jnp.minimum(jnp.maximum(result, -limit), limit).astype(held_as)


def gaussian_with(own_key, extent, width, reach, cuts, heavy, kind=jnp.bfloat16):
    drawn = width * jax.random.normal(own_key, extent, jnp.float32)
    if cuts:
        drawn = drawn * levels(own_key, extent, cuts, -0.22, 0.18)
    return jnp.clip(raised(drawn, jax.random.fold_in(own_key, 3), *heavy), -reach, reach).astype(kind)


def setup_inputs(seed: int = 0) -> dict:
    arg_keys = jax.random.split(jax.random.key(seed), 8)
    return {
        "tokens": gaussian_with(arg_keys[0], (TOKENS, D), 1.0, 6.0, ((0, 32),), (0, 1, 32, 2.75)),
        "routes": draw_routes(jax.random.fold_in(arg_keys[7], 71), 0),
        "gate_scale": jnp.clip(jnp.exp(math.log(2.0) - 2.3025851 * jax.random.uniform(arg_keys[2], (TOKENS, TOP), jnp.float32) ** levels(arg_keys[2], (TOKENS, TOP), ((0, 32),), -0.2, 0.2)), 0.2, 2.0),
        "w_gate": normal_values(arg_keys[3], (WINDOW, D, H), D ** -0.5, 0.125, ((0, 2), (1, 16))),
        "w_up": normal_values(arg_keys[4], (WINDOW, D, H), D ** -0.5, 0.125, ((0, 2), (1, 16))),
        "w_down": normal_values(arg_keys[5], (WINDOW, D, H), H ** -0.5, 0.21875, ((0, 2), (1, 16))),
        "d_out": gaussian_with(arg_keys[6], (TOKENS, D), 1.0, 6.0, ((0, 32),), (0, 1, 32, 2.75)),
    }


def reference(tokens, routes, gate_scale, w_gate, w_up, w_down, d_out):
    blocks = TOKENS // TOK_DEV
    slots = WINDOW * CAP
    per_block = TOK_DEV * TOP
    groups = blocks // WINDOW
    combine = gate_scale / jnp.sum(gate_scale, axis=1, keepdims=True)
    ids = routes.reshape(blocks, per_block)
    route_weight = combine.reshape(blocks, per_block)
    live = ids < WINDOW
    onehot = ((ids[:, :, None] == jnp.arange(WINDOW, dtype=jnp.int32)[None, None, :]) & live[:, :, None]).astype(jnp.int32)
    position = jnp.sum((jnp.cumsum(onehot, axis=1) - onehot) * onehot, axis=2)
    dest = jnp.where(live, ids * CAP + position, slots).astype(jnp.int32)
    block_idx = jnp.broadcast_to(jnp.arange(blocks, dtype=jnp.int32)[:, None], dest.shape)
    token_idx = block_idx * TOK_DEV + (jnp.arange(per_block, dtype=jnp.int32) // TOP)[None, :]
    source = jnp.zeros((blocks, slots + 1), jnp.int32).at[block_idx, dest].set(token_idx)[:, :slots]
    filled = jnp.zeros((blocks, slots + 1), jnp.int32).at[block_idx, dest].set(1)[:, :slots]
    slot_weight = jnp.zeros((blocks, slots + 1), jnp.float32).at[block_idx, dest].set(route_weight)[:, :slots]

    def regroup(values):
        return values.reshape(groups, WINDOW, WINDOW, CAP).transpose(2, 0, 1, 3).reshape(WINDOW, groups, WINDOW * CAP)

    source = regroup(source)
    filled = regroup(filled)
    slot_weight = regroup(slot_weight)

    def expert(index):
        src = source[index]
        used = filled[index][:, :, None] > 0
        x_rows = jnp.where(used, tokens[src], jnp.zeros((), jnp.bfloat16)).astype(jnp.bfloat16)
        d_rows = jnp.where(used, d_out[src].astype(jnp.float32) * slot_weight[index][:, :, None], 0.0).astype(jnp.bfloat16)
        wg = w_gate[index].astype(jnp.float32)
        wu = w_up[index].astype(jnp.float32)
        wd = w_down[index].astype(jnp.float32)
        xf = x_rows.astype(jnp.float32)
        df = d_rows.astype(jnp.float32)
        gate = jnp.einsum("grd,dh->grh", xf, wg)
        up = jnp.einsum("grd,dh->grh", xf, wu)
        sig = jax.nn.sigmoid(gate)
        act = gate * sig
        hidden = (act * up).astype(jnp.bfloat16)
        hf = hidden.astype(jnp.float32)
        expert_out = jnp.einsum("grh,dh->grd", hf, wd).astype(jnp.bfloat16)
        d_hidden = jnp.einsum("grd,dh->grh", df, wd)
        d_gate = (d_hidden * up * sig * (1.0 + gate * (1.0 - sig))).astype(jnp.bfloat16)
        d_up = (d_hidden * act).astype(jnp.bfloat16)
        dgf = d_gate.astype(jnp.float32)
        duf = d_up.astype(jnp.float32)
        d_in = (jnp.einsum("grh,dh->grd", dgf, wg) + jnp.einsum("grh,dh->grd", duf, wu)).astype(jnp.bfloat16)
        part_gate = jnp.einsum("grd,grh->gdh", xf, dgf).astype(jnp.bfloat16).astype(jnp.float32)
        part_up = jnp.einsum("grd,grh->gdh", xf, duf).astype(jnp.bfloat16).astype(jnp.float32)
        part_down = jnp.einsum("grd,grh->gdh", df, hf).astype(jnp.bfloat16).astype(jnp.float32)
        return expert_out, d_in, jnp.sum(part_gate, axis=0), jnp.sum(part_up, axis=0), jnp.sum(part_down, axis=0)

    expert_out, d_in, grad_gate, grad_up, grad_down = lax.map(expert, jnp.arange(WINDOW, dtype=jnp.int32))
    rows = WINDOW * CAP
    owner_expert = dest // CAP
    owner_slot = dest % CAP
    group_of = block_idx // WINDOW
    source_of = block_idx % WINDOW
    flat_row = (owner_expert * groups + group_of) * rows + source_of * CAP + owner_slot
    flat_row = jnp.where(live, flat_row, 0).astype(jnp.int32).reshape(TOKENS, TOP)
    live_tok = live.reshape(TOKENS, TOP)
    weight_tok = jnp.where(live_tok, combine, 0.0)
    flat_out = expert_out.reshape(-1, D)
    flat_in = d_in.reshape(-1, D)
    total_out = jnp.zeros((TOKENS, D), jnp.float32)
    total_in = jnp.zeros((TOKENS, D), jnp.float32)
    for choice_index in range(TOP):
        rows_pick = flat_row[:, choice_index]
        total_out = total_out + weight_tok[:, choice_index:choice_index + 1] * flat_out[rows_pick].astype(jnp.float32)
        total_in = total_in + jnp.where(live_tok[:, choice_index:choice_index + 1], flat_in[rows_pick].astype(jnp.float32), 0.0)
    return total_out.astype(jnp.bfloat16), total_in.astype(jnp.bfloat16), grad_gate, grad_up, grad_down
```

```python
import jax
import jax.numpy as jnp
from jax import lax
from jax.experimental import pallas as pl
from jax.experimental.pallas import tpu as pltpu
from jax.sharding import PartitionSpec as P

CAP = 32
CORES = 2
HALVES = 2
VMEM_BYTES = 48 * 1024 * 1024

CONTRACT_LAST = (((1,), (1,)), ((), ()))
CONTRACT_FIRST = (((0,), (0,)), ((), ()))


def call(kernel, out_shape, args, scratch=(), flops=0):
    moved = sum(a.size * a.dtype.itemsize for a in args) + sum(
        o.size * o.dtype.itemsize for o in out_shape
    )
    return pl.pallas_call(
        kernel,
        out_shape=out_shape,
        in_specs=[pl.BlockSpec(memory_space=pltpu.SMEM)]
        + [pl.BlockSpec(memory_space=pltpu.VMEM)] * (len(args) - 1),
        out_specs=[pl.BlockSpec(memory_space=pltpu.VMEM)] * len(out_shape),
        scratch_shapes=list(scratch),
        compiler_params=pltpu.CompilerParams(vmem_limit_bytes=VMEM_BYTES),
        cost_estimate=pl.CostEstimate(flops=flops, bytes_accessed=moved, transcendentals=0),
    )(*args)


def matches(routes, expert):
    return jnp.sum(jnp.where(routes == expert, 1.0, 0.0), axis=1, keepdims=True)


def chosen(routes, scale, expert):
    count = routes.shape[0]
    hit = matches(routes, expert)
    row = lax.broadcasted_iota(jnp.int32, (count, count), 0)
    column = lax.broadcasted_iota(jnp.int32, (count, count), 1)
    earlier = jnp.where(column < row, 1.0, 0.0).astype(jnp.bfloat16)
    place = jnp.dot(
        earlier,
        jnp.broadcast_to(hit, (count, 128)).astype(jnp.bfloat16),
        preferred_element_type=jnp.float32,
    )
    place = jnp.where(hit > 0.0, place[:, :1], -1.0).astype(jnp.int32)
    total = jnp.sum(scale, axis=1, keepdims=True)
    weight = jnp.sum(jnp.where(routes == expert, scale / total, 0.0), axis=1, keepdims=True)
    return place, weight


def selector(place):
    slots = lax.broadcasted_iota(jnp.int32, (place.shape[0], CAP), 1)
    return jnp.where(slots == place, 1.0, 0.0)


def shards(tokens, routes, gate_scale, w_gate, w_up, w_down, d_out):
    experts = lax.axis_size("expert")
    members = lax.axis_size("dp")
    chips = members // (HALVES * CORES)
    count, width = tokens.shape
    span = width // HALVES
    block, inner = w_gate.shape[1:]
    rows = experts * CAP
    bf16, f32 = jnp.bfloat16, jnp.float32
    spots = [(h, s) for h in range(HALVES) for s in range(experts)]

    member = lax.axis_index("dp")
    here = jnp.stack(
        [
            member // (chips * CORES),
            member // CORES % chips,
            member % CORES,
            lax.axis_index("expert"),
        ]
    ).astype(jnp.int32)

    def send(value, half=0, chip=0, core=0, shift=0):
        perm = []
        for d in range(members):
            to = d ^ (half * chips * CORES + chip * CORES + core)
            for e in range(experts):
                perm.append((d * experts + e, to * experts + (e + shift) % experts))
        return lax.ppermute(value, ("dp", "expert"), perm)

    def shape(*dims, dtype=bf16):
        return jax.ShapeDtypeStruct(dims, dtype)

    packed = jnp.concatenate([w_gate, w_up, w_down], axis=0)
    mine = [packed] + [send(packed, chip=o) for o in range(1, chips)]

    def dispatch(at, r_ref, s_ref, t_ref, d_ref, *outs):
        route, scale = r_ref[...], s_ref[...]
        for s in range(experts):
            expert = lax.rem(at[3] + s, experts)
            place, weight = chosen(route, scale, expert)
            pick = selector(place).astype(bf16)
            for h in range(HALVES):
                side = jnp.bitwise_xor(at[0], h)
                cols = pl.ds(pl.multiple_of(side * span, span), span)
                scaled = (d_ref[:, cols].astype(f32) * weight).astype(bf16)
                out = outs[h * experts + s]
                out[0] = lax.dot_general(
                    pick, t_ref[:, cols], CONTRACT_FIRST, preferred_element_type=f32
                ).astype(bf16)
                out[1] = lax.dot_general(
                    pick, scaled, CONTRACT_FIRST, preferred_element_type=f32
                ).astype(bf16)
            outs[-2][:, s : s + 1] = place
            outs[-1][:, s : s + 1] = weight

    *cut, places, weights = call(
        dispatch,
        [shape(2, CAP, span)] * len(spots)
        + [shape(count, experts, dtype=jnp.int32), shape(count, experts, dtype=f32)],
        [here, routes, gate_scale, tokens, d_out],
    )
    pieces = [cut[0]] + [
        send(cut[i], half=h, shift=s) for i, (h, s) in enumerate(spots) if i > 0
    ]
    theirs = [send(m, core=1) for m in mine]

    def gather_weights(at, refs, held):
        for i, ref in enumerate(refs):
            chip, core = i % chips, i // chips
            start = (jnp.bitwise_xor(at[1], chip) * CORES + jnp.bitwise_xor(at[2], core)) * block
            for m in range(3):
                held[m, pl.ds(pl.multiple_of(start, block), block), :] = ref[m]

    def project(at, *refs):
        ins, refs = refs[: len(spots)], refs[len(spots) :]
        ws, refs = refs[: chips * CORES], refs[chips * CORES :]
        keep, give, stay, leave, held = refs
        gather_weights(at, ws, held)
        x = jnp.concatenate([ref[0] for ref in ins], axis=0)
        d = jnp.concatenate([ref[1] for ref in ins], axis=0)
        for m, left in enumerate((x, x, d)):
            part = jnp.dot(left, held[m], preferred_element_type=f32)
            keep[m] = part[:rows]
            give[m] = part[rows:].astype(bf16)
        first = at[2] == 0
        for k in range(2):
            for i, ref in enumerate(ins):
                for chip in range(chips):
                    both = ref[k, :, chip * CORES * block : (chip + 1) * CORES * block]
                    low, high = both[:, :block], both[:, block:]
                    place = (k, slice(i * CAP, (i + 1) * CAP), slice(chip * block, (chip + 1) * block))
                    stay[place] = jnp.where(first, low, high)
                    leave[place] = jnp.where(first, high, low)

    keep, give, stay, leave = call(
        project,
        [
            shape(3, rows, inner, dtype=f32),
            shape(3, rows, inner),
            shape(2, HALVES * rows, chips * block),
            shape(2, HALVES * rows, chips * block),
        ],
        [here, *pieces, *mine, *theirs],
        scratch=[pltpu.VMEM((3, span, inner), bf16)],
        flops=2 * 3 * HALVES * rows * span * inner,
    )
    came = send(give, half=1)
    across = send(leave, core=1)

    def activate(at, keep_ref, came_ref, out):
        gate = keep_ref[0] + came_ref[0].astype(f32)
        up = keep_ref[1] + came_ref[1].astype(f32)
        d_hidden = keep_ref[2] + came_ref[2].astype(f32)
        sig = jax.nn.sigmoid(gate)
        act = gate * sig
        out[0] = (d_hidden * up * sig * (1.0 + gate * (1.0 - sig))).astype(bf16)
        out[1] = (d_hidden * act).astype(bf16)
        out[2] = (act * up).astype(bf16)

    (inside,) = call(activate, [shape(3, rows, inner)], [here, keep, came])
    other = send(inside, half=1)
    inside_c = send(inside, core=1)
    other_c = send(other, core=1)

    def weigh(at, a0, a1, a2, a3, x0, x1, *refs):
        outs, held = refs[:-1], refs[-1]
        for m in range(3):
            left = jnp.concatenate([x0[m // 2], x1[m // 2]], axis=0)
            right = jnp.concatenate([a0[m], a1[m], a2[m], a3[m]], axis=0)
            held[...] = lax.dot_general(left, right, CONTRACT_FIRST, preferred_element_type=f32)
            for o, out in enumerate(outs):
                start = pl.multiple_of(jnp.bitwise_xor(at[1], o) * block, block)
                out[m] = held[pl.ds(start, block), :].astype(out.dtype)

    grads = call(
        weigh,
        [shape(3, block, inner, dtype=f32)] + [shape(3, block, inner)] * (chips - 1),
        [here, inside, other, inside_c, other_c, stay, across],
        scratch=[pltpu.VMEM((chips * block, inner), f32)],
        flops=2 * 3 * CORES * HALVES * rows * chips * block * inner,
    )
    arrived = [send(grads[o], chip=o) for o in range(1, chips)]

    def expand(at, a0, a1, *refs):
        ws, outs, held = refs[: chips * CORES], refs[chips * CORES : -1], refs[-1]
        gather_weights(at, ws, held)
        part = [jnp.concatenate([a0[m], a1[m]], axis=0) for m in range(3)]
        out = lax.dot_general(part[2], held[2], CONTRACT_LAST, preferred_element_type=f32)
        d_in = lax.dot_general(
            part[0], held[0], CONTRACT_LAST, preferred_element_type=f32
        ) + lax.dot_general(part[1], held[1], CONTRACT_LAST, preferred_element_type=f32)
        for i, ref in enumerate(outs):
            ref[0] = out[i * CAP : (i + 1) * CAP].astype(bf16)
            ref[1] = d_in[i * CAP : (i + 1) * CAP].astype(bf16)

    back = call(
        expand,
        [shape(2, CAP, span)] * len(spots),
        [here, inside, other, *mine, *theirs],
        scratch=[pltpu.VMEM((3, span, inner), bf16)],
        flops=2 * 3 * HALVES * rows * span * inner,
    )
    home = [back[0]] + [
        send(back[i], half=h, shift=-s) for i, (h, s) in enumerate(spots) if i > 0
    ]

    def collect(at, p_ref, w_ref, *refs):
        ins, (out, d_in) = refs[: len(spots)], refs[len(spots) :]
        picks = [selector(p_ref[:, s : s + 1]).astype(bf16) for s in range(experts)]
        for h in range(HALVES):
            side = jnp.bitwise_xor(at[0], h)
            cols = pl.ds(pl.multiple_of(side * span, span), span)
            total_out = jnp.zeros((count, span), f32)
            total_in = jnp.zeros((count, span), f32)
            for s in range(experts):
                ref = ins[h * experts + s]
                total_out += w_ref[:, s : s + 1] * jnp.dot(
                    picks[s], ref[0], preferred_element_type=f32
                )
                total_in += jnp.dot(picks[s], ref[1], preferred_element_type=f32)
            out[:, cols] = total_out.astype(bf16)
            d_in[:, cols] = total_in.astype(bf16)

    layer_out, d_tokens = call(
        collect, [shape(count, width)] * 2, [here, places, weights, *home]
    )

    def finish(at, own, *refs):
        ins, outs = refs[: chips - 1], refs[chips - 1 :]
        for m, out in enumerate(outs):
            total = own[m]
            for ref in ins:
                total = total + ref[m].astype(f32)
            out[0] = total

    grad_gate, grad_up, grad_down = call(
        finish, [shape(1, block, inner, dtype=f32)] * 3, [here, grads[0], *arrived]
    )
    return layer_out, d_tokens, grad_gate, grad_up, grad_down


def solution(mesh):
    by_token = P(("dp", "expert"), None)
    by_expert = P("expert", "dp", None)
    return jax.shard_map(
        shards,
        mesh=mesh,
        in_specs=(by_token,) * 3 + (by_expert,) * 3 + (by_token,),
        out_specs=(by_token,) * 2 + (by_expert,) * 3,
        check_vma=False,
    )
```

```python
import functools

import jax
import jax.numpy as jnp
from jax import lax
from jax.experimental import pallas as pl
from jax.experimental.pallas import tpu as pltpu
from jax.sharding import PartitionSpec as P

CAP = 32
CORES = 2
HALVES = 2
VMEM_BYTES = 48 * 1024 * 1024

CONTRACT_LAST = (((1,), (1,)), ((), ()))
CONTRACT_FIRST = (((0,), (0,)), ((), ()))


def call(kernel, out_shape, args, scratch=(), flops=0):
    moved = sum(a.size * a.dtype.itemsize for a in args) + sum(
        o.size * o.dtype.itemsize for o in out_shape
    )
    return pl.pallas_call(
        kernel,
        out_shape=out_shape,
        in_specs=[pl.BlockSpec(memory_space=pltpu.SMEM)]
        + [pl.BlockSpec(memory_space=pltpu.VMEM)] * (len(args) - 1),
        out_specs=[pl.BlockSpec(memory_space=pltpu.VMEM)] * len(out_shape),
        scratch_shapes=list(scratch),
        compiler_params=pltpu.CompilerParams(vmem_limit_bytes=VMEM_BYTES),
        cost_estimate=pl.CostEstimate(flops=flops, bytes_accessed=moved, transcendentals=0),
    )(*args)


def rank(hits):
    count = hits.shape[1]
    row = lax.broadcasted_iota(jnp.int32, (count, count), 0)
    column = lax.broadcasted_iota(jnp.int32, (count, count), 1)
    earlier = jnp.where(row < column, 1.0, 0.0).astype(jnp.bfloat16)
    return jnp.dot(hits.astype(jnp.bfloat16), earlier, preferred_element_type=jnp.float32)


def selector(place):
    slots = lax.broadcasted_iota(jnp.int32, (CAP, place.shape[1]), 0).astype(jnp.float32)
    return jnp.where(slots == place, 1.0, 0.0)


def shards(tokens, routes, gate_scale, w_gate, w_up, w_down, d_out):
    experts = lax.axis_size("expert")
    members = lax.axis_size("dp")
    chips = members // (HALVES * CORES)
    count, width = tokens.shape
    span = width // HALVES
    block, inner = w_gate.shape[1:]
    rows = experts * CAP
    bf16, f32 = jnp.bfloat16, jnp.float32
    spots = [(h, s) for h in range(HALVES) for s in range(experts)]

    member = lax.axis_index("dp")
    here = jnp.stack(
        [
            member // (chips * CORES),
            member // CORES % chips,
            member % CORES,
            lax.axis_index("expert"),
        ]
    ).astype(jnp.int32)

    def send(value, half=0, chip=0, core=0, shift=0):
        perm = []
        for d in range(members):
            to = d ^ (half * chips * CORES + chip * CORES + core)
            for e in range(experts):
                perm.append((d * experts + e, to * experts + (e + shift) % experts))
        return lax.ppermute(value, ("dp", "expert"), perm)

    def shape(*dims, dtype=bf16):
        return jax.ShapeDtypeStruct(dims, dtype)

    half_block = block // 2

    def pack(g_ref, u_ref, w_ref, out):
        for m, ref in enumerate((g_ref, u_ref, w_ref)):
            for k in range(2):
                out[k, m] = ref[0, k * half_block : (k + 1) * half_block]

    own = pl.pallas_call(pack, out_shape=shape(2, 3, half_block, inner))(w_gate, w_up, w_down)
    two_hops = chips == 4
    near = [send(own, chip=o) for o in range(1, chips - 1 if two_hops else chips)]
    own_c = send(own, core=1)

    def dispatch(at, r_ref, s_ref, t_ref, d_ref, *outs):
        *outs, p_ref, c_ref = outs
        route, scale = r_ref[...], s_ref[...]
        combine = scale / jnp.sum(scale, axis=0, keepdims=True)
        hits, weights = [], []
        for s in range(experts):
            match = route == lax.rem(at[3] + s, experts)
            hits.append(jnp.sum(jnp.where(match, 1.0, 0.0), axis=0, keepdims=True))
            weights.append(jnp.sum(jnp.where(match, combine, 0.0), axis=0, keepdims=True))
        pad = [jnp.zeros((8 - experts, count), f32)] if experts < 8 else []
        hits = jnp.concatenate(hits + pad, axis=0)
        places = jnp.where(hits > 0.0, rank(hits), -1.0)
        p_ref[...] = places
        c_ref[...] = jnp.concatenate(weights + pad, axis=0)
        for s in range(experts):
            pick = selector(places[s : s + 1])
            weight = jnp.sum(pick * weights[s], axis=1, keepdims=True)
            pick = pick.astype(bf16)
            for h in range(HALVES):
                side = jnp.bitwise_xor(at[0], h)
                cols = pl.ds(pl.multiple_of(side * span, span), span)
                out = outs[s].at[h]
                out[0] = jnp.dot(pick, t_ref[:, cols], preferred_element_type=f32).astype(bf16)
                out[1] = (
                    jnp.dot(pick, d_ref[:, cols], preferred_element_type=f32) * weight
                ).astype(bf16)

    *cut, places, weights = call(
        dispatch,
        [shape(HALVES, 2, CAP, span)] * experts + [shape(max(experts, 8), count, dtype=f32)] * 2,
        [here, routes.T, gate_scale.T, tokens, d_out],
    )
    *cut, own_c = lax.optimization_barrier((*cut, own_c))
    lead = [cut[0]] + [send(cut[s], shift=s) for s in range(1, experts)]
    follow = [send(m[1], half=1) for m in lead]
    pieces = [m[0] for m in lead] + follow

    *near, pieces[experts] = lax.optimization_barrier((*near, pieces[experts]))
    if two_hops:
        far = [send(near[0][0], chip=2), send(near[1][1], chip=1)]
    else:
        far = []
    *far, pieces = lax.optimization_barrier((*far, tuple(pieces)))
    here_blocks = [own] + near + far
    there_blocks = [own_c] + [send(m, core=1) for m in near + far]
    blocks = here_blocks + there_blocks

    def assemble(at, refs, held, kinds):
        for i, ref in enumerate(refs):
            core, place = divmod(i, len(here_blocks))
            for k in range(2):
                if len(ref.shape) == 4:
                    chip, part = place, ref.at[k]
                elif place - chips + 1 == k:
                    chip, part = chips - 1, ref
                else:
                    continue
                owner = jnp.bitwise_xor(at[1], chip) * CORES + jnp.bitwise_xor(at[2], core)
                start = pl.multiple_of(owner * block + k * half_block, half_block)
                for m, kind in enumerate(kinds):
                    held[m, pl.ds(start, half_block), :] = part[kind]

    def project(at, *refs):
        ins, refs = refs[: len(spots)], refs[len(spots) :]
        ws, (keep, give, held) = refs[: len(blocks)], refs[len(blocks) :]
        assemble(at, ws, held, (0, 1, 2))
        for m, side in enumerate((0, 0, 1)):
            left = jnp.concatenate([ref[side] for ref in ins], axis=0)
            part = jnp.dot(left, held[m], preferred_element_type=f32)
            keep[m] = part[:rows]
            give[m] = part[rows:].astype(bf16)

    keep, give = call(
        project,
        [shape(3, rows, inner, dtype=f32), shape(3, rows, inner)],
        [here, *pieces, *blocks],
        scratch=[pltpu.VMEM((3, span, inner), bf16)],
        flops=2 * 3 * HALVES * rows * span * inner,
    )
    came = send(give, half=1)

    def divide(at, *refs):
        ins, (stay, leave) = refs[: len(spots)], refs[len(spots) :]
        first = at[2] == 0
        for k in range(2):
            for i, ref in enumerate(ins):
                for chip in range(chips):
                    both = ref[k, :, chip * CORES * block : (chip + 1) * CORES * block]
                    low, high = both[:, :block], both[:, block:]
                    place = (k, slice(i * CAP, (i + 1) * CAP), slice(chip * block, (chip + 1) * block))
                    stay[place] = jnp.where(first, low, high)
                    leave[place] = jnp.where(first, high, low)

    stay, leave = call(
        divide, [shape(2, HALVES * rows, chips * block)] * 2, [here, *pieces]
    )
    across = send(leave, core=1)

    came, across = lax.optimization_barrier((came, across))

    def activate(at, keep_ref, came_ref, out):
        gate = keep_ref[0] + came_ref[0].astype(f32)
        up = keep_ref[1] + came_ref[1].astype(f32)
        d_hidden = keep_ref[2] + came_ref[2].astype(f32)
        sig = jax.nn.sigmoid(gate)
        act = gate * sig
        out[0] = (d_hidden * up * sig * (1.0 + gate * (1.0 - sig))).astype(bf16)
        out[1] = (d_hidden * act).astype(bf16)
        out[2] = (act * up).astype(bf16)

    (inside,) = call(activate, [shape(3, rows, inner)], [here, keep, came])
    other = send(inside, half=1)
    inside_c = send(inside, core=1)

    def weigh(at, a0, a1, a2, a3, x0, x1, *refs):
        outs, held = refs[:-1], refs[-1]
        for m in range(3):
            left = jnp.concatenate([x0[m // 2], x1[m // 2]], axis=0)
            right = jnp.concatenate([a0[m], a1[m], a2[m], a3[m]], axis=0)
            held[...] = lax.dot_general(left, right, CONTRACT_FIRST, preferred_element_type=f32)
            for o, out in enumerate(outs):
                start = pl.multiple_of(jnp.bitwise_xor(at[1], o) * block, block)
                out[m] = held[pl.ds(start, block), :].astype(out.dtype)

    other_c = send(other, core=1)

    def expand(at, a0, a1, *refs):
        ws, (*outs, held) = refs[: len(blocks)], refs[len(blocks) :]
        assemble(at, ws, held, (0, 1, 2))
        left = [jnp.concatenate([a0[m], a1[m]], axis=0) for m in range(3)]
        out = lax.dot_general(left[2], held[2], CONTRACT_LAST, preferred_element_type=f32)
        d_in = lax.dot_general(
            left[0], held[0], CONTRACT_LAST, preferred_element_type=f32
        ) + lax.dot_general(left[1], held[1], CONTRACT_LAST, preferred_element_type=f32)
        for s in range(experts):
            for h in range(HALVES):
                part = slice((h * experts + s) * CAP, (h * experts + s + 1) * CAP)
                ref = outs[s] if h == 0 else outs[experts].at[s]
                ref[0] = out[part].astype(bf16)
                ref[1] = d_in[part].astype(bf16)

    *back, far_back = call(
        expand,
        [shape(2, CAP, span)] * experts + [shape(experts, 2, CAP, span)],
        [here, inside, other, *blocks],
        scratch=[pltpu.VMEM((3, span, inner), bf16)],
        flops=2 * 3 * HALVES * rows * span * inner,
    )
    back, inside_c = lax.optimization_barrier((back, inside_c))
    grads = call(
        weigh,
        [shape(3, block, inner, dtype=f32)] + [shape(3, block, inner)] * (chips - 1),
        [here, inside, other, inside_c, other_c, stay, across],
        scratch=[pltpu.VMEM((chips * block, inner), f32)],
        flops=2 * 3 * CORES * HALVES * rows * chips * block * inner,
    )
    grads = [grads[0]] + [send(grads[o], chip=o) for o in range(1, chips)]
    far_back = send(far_back, half=1)
    home = [back[0]] + [send(back[s], shift=-s) for s in range(1, experts)]
    home += [far_back[0]] + [send(far_back[s], shift=-s) for s in range(1, experts)]

    def collect(at, p_ref, w_ref, *refs):
        ins, (out, d_in) = refs[: len(spots)], refs[len(spots) :]
        picks = [selector(p_ref[s : s + 1]).astype(bf16) for s in range(experts)]
        columns = jnp.transpose(w_ref[...])
        for h in range(HALVES):
            side = jnp.bitwise_xor(at[0], h)
            cols = pl.ds(pl.multiple_of(side * span, span), span)
            total_out = jnp.zeros((count, span), f32)
            total_in = jnp.zeros((count, span), f32)
            for s in range(experts):
                ref = ins[h * experts + s]
                total_out += columns[:, s : s + 1] * lax.dot_general(
                    picks[s], ref[0], CONTRACT_FIRST, preferred_element_type=f32
                )
                total_in += lax.dot_general(
                    picks[s], ref[1], CONTRACT_FIRST, preferred_element_type=f32
                )
            out[:, cols] = total_out.astype(bf16)
            d_in[:, cols] = total_in.astype(bf16)

    layer_out, d_tokens = call(
        collect, [shape(count, width)] * 2, [here, places, weights, *home]
    )

    d_tokens, grads = lax.optimization_barrier((d_tokens, grads))

    def finish(at, own, *refs):
        ins, outs = refs[: chips - 1], refs[chips - 1 :]
        for m, out in enumerate(outs):
            total = own[m]
            for ref in ins:
                total = total + ref[m].astype(f32)
            out[0] = total

    grad_gate, grad_up, grad_down = call(
        finish, [shape(1, block, inner, dtype=f32)] * 3, [here, *grads]
    )
    return layer_out, d_tokens, grad_gate, grad_up, grad_down


def solution(mesh):
    by_token = P(("dp", "expert"), None)
    by_expert = P("expert", "dp", None)
    return jax.shard_map(
        shards,
        mesh=mesh,
        in_specs=(by_token,) * 3 + (by_expert,) * 3 + (by_token,),
        out_specs=(by_token,) * 2 + (by_expert,) * 3,
        check_vma=False,
    )
```

```python
import functools

import jax
import jax.numpy as jnp
from jax import lax
from jax.experimental import pallas as pl
from jax.experimental.pallas import tpu as pltpu
from jax.sharding import PartitionSpec as P

CAP = 32
CORES = 2
HALVES = 2
PARTS = 2
VMEM_BYTES = 48 * 1024 * 1024

CONTRACT_LAST = (((1,), (1,)), ((), ()))
CONTRACT_FIRST = (((0,), (0,)), ((), ()))


def call(kernel, out_shape, args, scratch=(), flops=0, positions=True):
    moved = sum(a.size * a.dtype.itemsize for a in args) + sum(
        o.size * o.dtype.itemsize for o in out_shape
    )
    return pl.pallas_call(
        kernel,
        out_shape=out_shape,
        in_specs=[
            pl.BlockSpec(memory_space=pltpu.SMEM if positions and i == 0 else pltpu.VMEM)
            for i in range(len(args))
        ],
        out_specs=[pl.BlockSpec(memory_space=pltpu.VMEM)] * len(out_shape),
        scratch_shapes=list(scratch),
        compiler_params=pltpu.CompilerParams(vmem_limit_bytes=VMEM_BYTES),
        cost_estimate=pl.CostEstimate(flops=flops, bytes_accessed=moved, transcendentals=0),
    )(*args)


def rank(hits):
    count = hits.shape[1]
    row = lax.broadcasted_iota(jnp.int32, (count, count), 0)
    column = lax.broadcasted_iota(jnp.int32, (count, count), 1)
    earlier = jnp.where(row < column, 1.0, 0.0).astype(jnp.bfloat16)
    return jnp.dot(hits.astype(jnp.bfloat16), earlier, preferred_element_type=jnp.float32)


def selector(place):
    slots = lax.broadcasted_iota(jnp.int32, (CAP, place.shape[1]), 0).astype(jnp.float32)
    return jnp.where(slots == place, 1.0, 0.0)


def shards(tokens, routes, gate_scale, w_gate, w_up, w_down, d_out):
    experts = lax.axis_size("expert")
    members = lax.axis_size("dp")
    chips = members // (HALVES * CORES)
    count, width = tokens.shape
    span = width // HALVES
    block, inner = w_gate.shape[1:]
    rows = experts * CAP
    bf16, f32 = jnp.bfloat16, jnp.float32
    spots = [(h, s) for h in range(HALVES) for s in range(experts)]

    member = lax.axis_index("dp")
    here = jnp.stack(
        [
            member // (chips * CORES),
            member // CORES % chips,
            member % CORES,
            lax.axis_index("expert"),
        ]
    ).astype(jnp.int32)

    def send(value, half=0, chip=0, core=0, shift=0):
        perm = []
        for d in range(members):
            to = d ^ (half * chips * CORES + chip * CORES + core)
            for e in range(experts):
                perm.append((d * experts + e, to * experts + (e + shift) % experts))
        return lax.ppermute(value, ("dp", "expert"), perm)

    def shape(*dims, dtype=bf16):
        return jax.ShapeDtypeStruct(dims, dtype)

    half_block = block // 2
    strip = inner // PARTS
    two_hops = chips == 4

    def pack(g_ref, u_ref, w_ref, *outs):
        for m, ref in enumerate((g_ref, u_ref, w_ref)):
            for k in range(2):
                for i, out in enumerate(outs):
                    out[k, m] = ref[
                        0, k * half_block : (k + 1) * half_block, i * strip : (i + 1) * strip
                    ]

    owns = list(
        pl.pallas_call(pack, out_shape=[shape(2, 3, half_block, strip)] * PARTS)(
            w_gate, w_up, w_down
        )
    )

    def first_hop(own):
        return [send(own, chip=o) for o in range(1, chips - 1 if two_hops else chips)]

    def second_hop(near):
        return [send(near[0][0], chip=2), send(near[1][1], chip=1)] if two_hops else []

    near = first_hop(owns[0])
    own_c = send(owns[0], core=1)

    def dispatch(at, r_ref, s_ref, t_ref, d_ref, *outs):
        *outs, p_ref, c_ref = outs
        route, scale = r_ref[...], s_ref[...]
        combine = scale / jnp.sum(scale, axis=0, keepdims=True)
        hits, weights = [], []
        for s in range(experts):
            match = route == lax.rem(at[3] + s, experts)
            hits.append(jnp.sum(jnp.where(match, 1.0, 0.0), axis=0, keepdims=True))
            weights.append(jnp.sum(jnp.where(match, combine, 0.0), axis=0, keepdims=True))
        pad = [jnp.zeros((8 - experts, count), f32)] if experts < 8 else []
        hits = jnp.concatenate(hits + pad, axis=0)
        places = jnp.where(hits > 0.0, rank(hits), -1.0)
        p_ref[...] = places
        c_ref[...] = jnp.concatenate(weights + pad, axis=0)
        for s in range(experts):
            pick = selector(places[s : s + 1])
            weight = jnp.sum(pick * weights[s], axis=1, keepdims=True)
            pick = pick.astype(bf16)
            for h in range(HALVES):
                side = jnp.bitwise_xor(at[0], h)
                cols = pl.ds(pl.multiple_of(side * span, span), span)
                out = outs[s].at[h]
                out[0] = jnp.dot(pick, t_ref[:, cols], preferred_element_type=f32).astype(bf16)
                out[1] = (
                    jnp.dot(pick, d_ref[:, cols], preferred_element_type=f32) * weight
                ).astype(bf16)

    *cut, places, weights = call(
        dispatch,
        [shape(HALVES, 2, CAP, span)] * experts + [shape(max(experts, 8), count, dtype=f32)] * 2,
        [here, routes.T, gate_scale.T, tokens, d_out],
    )
    *cut, own_c = lax.optimization_barrier((*cut, own_c))
    lead = [cut[0]] + [send(cut[s], shift=s) for s in range(1, experts)]
    follow = [send(m[1], half=1) for m in lead]
    pieces = [m[0] for m in lead] + follow

    *near, pieces[experts] = lax.optimization_barrier((*near, pieces[experts]))
    far = second_hop(near)
    reach = len(owns[:1]) + len(near) + len(far)
    parts = [[owns[0], *near, *far, own_c] + [send(m, core=1) for m in near + far]]
    for i in range(1, PARTS):
        owns[i], far = lax.optimization_barrier((owns[i], far or near[-1:]))
        near = first_hop(owns[i])
        far = second_hop(near)
        mine = [owns[i], *near, *far]
        parts.append(mine + [send(m, core=1) for m in mine])

    def assemble(at, refs, held, column):
        for i, ref in enumerate(refs):
            core, place = divmod(i, reach)
            for k in range(2):
                if len(ref.shape) == 4:
                    chip, part = place, ref.at[k]
                elif place - chips + 1 == k:
                    chip, part = chips - 1, ref
                else:
                    continue
                owner = jnp.bitwise_xor(at[1], chip) * CORES + jnp.bitwise_xor(at[2], core)
                start = pl.multiple_of(owner * block + k * half_block, half_block)
                for m in range(3):
                    held[m, pl.ds(start, half_block), column : column + strip] = part[m]

    def project(at, *refs):
        ins, refs = refs[: len(spots)], refs[len(spots) :]
        *ws, keep, give, held = refs
        assemble(at, ws, held, 0)
        for m, side in enumerate((0, 0, 1)):
            left = jnp.concatenate([ref[side] for ref in ins], axis=0)
            part = jnp.dot(left, held[m], preferred_element_type=f32)
            keep[m] = part
            give[m, :rows] = part[rows:].astype(bf16)
            give[m, rows:] = part[:rows].astype(bf16)

    keeps, gives = [], []
    for i in range(PARTS):
        keep, give = call(
            project,
            [shape(3, HALVES * rows, strip, dtype=f32), shape(3, HALVES * rows, strip)],
            [here, *pieces, *parts[i]],
            scratch=[pltpu.VMEM((3, span, strip), bf16)],
            flops=2 * 3 * HALVES * rows * span * strip,
        )
        keeps.append(keep)
        gives.append(give)
    cames = [send(gives[0], half=1)]

    def divide(at, *refs):
        ins, (stay, leave) = refs[: len(spots)], refs[len(spots) :]
        first = at[2] == 0
        for k in range(2):
            for i, ref in enumerate(ins):
                for chip in range(chips):
                    both = ref[k, :, chip * CORES * block : (chip + 1) * CORES * block]
                    low, high = both[:, :block], both[:, block:]
                    place = (k, slice(i * CAP, (i + 1) * CAP), slice(chip * block, (chip + 1) * block))
                    stay[place] = jnp.where(first, low, high)
                    leave[place] = jnp.where(first, high, low)

    keeps[0], apart = lax.optimization_barrier((keeps[0], tuple(pieces)))
    stay, leave = call(
        divide, [shape(2, HALVES * rows, chips * block)] * 2, [here, *apart]
    )
    across = send(leave, core=1)

    cames[0], across = lax.optimization_barrier((cames[0], across))
    for i in range(1, PARTS):
        cames.append(send(gives[i], half=1))

    def activate(at, keep_ref, came_ref, out):
        gate = keep_ref[0] + came_ref[0].astype(f32)
        up = keep_ref[1] + came_ref[1].astype(f32)
        d_hidden = keep_ref[2] + came_ref[2].astype(f32)
        sig = jax.nn.sigmoid(gate)
        act = gate * sig
        out[0] = (d_hidden * up * sig * (1.0 + gate * (1.0 - sig))).astype(bf16)
        out[1] = (d_hidden * act).astype(bf16)
        out[2] = (act * up).astype(bf16)

    low, high = slice(0, half_block), slice(half_block, block)

    def weigh(at, mine, theirs, x0, x1, *refs):
        outs, held = refs[:-1], refs[-1]
        for m in range(3):
            left = jnp.concatenate([x0[m // 2], x1[m // 2]], axis=0)
            right = jnp.concatenate([mine[m], theirs[m]], axis=0)
            held[...] = lax.dot_general(left, right, CONTRACT_FIRST, preferred_element_type=f32)

            def owned(o):
                start = pl.multiple_of(jnp.bitwise_xor(at[1], o) * block, block)
                return held[pl.ds(start, block), :]

            outs[0][m] = owned(0)
            if two_hops:
                _, by_first, by_second, kept = outs
                first, second, across_it = owned(1), owned(2), owned(3)
                by_first[0, m] = across_it[low].astype(bf16)
                by_first[1, m] = first[low].astype(bf16)
                by_second[0, m] = across_it[high].astype(bf16)
                by_second[1, m] = second[high].astype(bf16)
                kept[0, m] = second[low]
                kept[1, m] = first[high]
            else:
                for o in range(1, chips):
                    outs[o][m] = owned(o).astype(bf16)

    def weigh_with(mine, theirs):
        if two_hops:
            others = [shape(2, 3, half_block, strip)] * 2
            others.append(shape(2, 3, half_block, strip, dtype=f32))
        else:
            others = [shape(3, block, strip)] * (chips - 1)
        return list(
            call(
                weigh,
                [shape(3, block, strip, dtype=f32), *others],
                [here, mine, theirs, stay, across],
                scratch=[pltpu.VMEM((chips * block, strip), f32)],
                flops=2 * 3 * CORES * HALVES * rows * chips * block * strip,
            )
        )

    def relay(kept, from_first, from_second, to_second, to_first):
        to_second[...] = (kept[0] + from_first[0].astype(f32)).astype(bf16)
        to_first[...] = (kept[1] + from_second[0].astype(f32)).astype(bf16)

    def leave_first(grads):
        if two_hops:
            return [send(grads[1], chip=1), send(grads[2], chip=2)]
        return [send(grads[o], chip=o) for o in range(1, chips)]

    def join(grads, came):
        if not two_hops:
            return []
        return list(
            call(relay, [shape(3, half_block, strip)] * 2, [grads[3], *came], positions=False)
        )

    def leave_second(joined):
        return [send(m, chip=2 - i) for i, m in enumerate(joined)]

    inside, inside_c, arrived = [], [], []
    for i in range(PARTS):
        inside += call(
            activate, [shape(3, HALVES * rows, strip)], [here, keeps[i], cames[i]]
        )
        inside_c.append(send(inside[i], core=1))
        if i + 1 < PARTS:
            grads = weigh_with(inside[i], inside_c[i])
            grads[0], cames[i + 1] = lax.optimization_barrier((grads[0], cames[i + 1]))
            hop = leave_first(grads)
            hop[0], cames[i + 1] = lax.optimization_barrier((hop[0], cames[i + 1]))
            joined = join(grads, hop)
            arrived.append([grads[0], *hop, *leave_second(joined)])

    def expand(at, *refs):
        count_outs = HALVES * experts + 1
        ins, ws, (*outs, held) = refs[:PARTS], refs[PARTS:-count_outs], refs[-count_outs:]
        for i in range(PARTS):
            assemble(at, ws[i * len(parts[0]) : (i + 1) * len(parts[0])], held, i * strip)
        left = [jnp.concatenate([ref[m] for ref in ins], axis=1) for m in range(3)]
        out = lax.dot_general(left[2], held[2], CONTRACT_LAST, preferred_element_type=f32)
        d_in = lax.dot_general(
            left[0], held[0], CONTRACT_LAST, preferred_element_type=f32
        ) + lax.dot_general(left[1], held[1], CONTRACT_LAST, preferred_element_type=f32)
        for s in range(experts):
            for h in range(HALVES):
                part = slice((h * experts + s) * CAP, (h * experts + s + 1) * CAP)
                ref = outs[h * experts + s]
                ref[0] = out[part].astype(bf16)
                ref[1] = d_in[part].astype(bf16)

    back = call(
        expand,
        [shape(2, CAP, span)] * len(spots),
        [here, *inside, *sum(parts, [])],
        scratch=[pltpu.VMEM((3, span, inner), bf16)],
        flops=2 * 3 * HALVES * rows * span * inner,
    )
    *back, inside_c[-1] = lax.optimization_barrier((*back, inside_c[-1]))
    last = weigh_with(inside[-1], inside_c[-1])
    hop = leave_first(last)
    joined = join(last, hop)
    home = {(0, 0): back[0]}
    for i, (h, s) in enumerate(spots):
        if h > 0:
            home[h, s] = send(back[i], half=h, shift=-s)
    joined, near_back = lax.optimization_barrier((joined, tuple(back[1:experts])))
    for s in range(1, experts):
        home[0, s] = send(near_back[s - 1], shift=-s)
    home = [home[spot] for spot in spots]
    arrived.append([last[0], *hop, *leave_second(joined)])

    def collect(at, p_ref, w_ref, *refs):
        ins, (out, d_in) = refs[: len(spots)], refs[len(spots) :]
        picks = [selector(p_ref[s : s + 1]).astype(bf16) for s in range(experts)]
        columns = jnp.transpose(w_ref[...])
        for h in range(HALVES):
            side = jnp.bitwise_xor(at[0], h)
            cols = pl.ds(pl.multiple_of(side * span, span), span)
            total_out = jnp.zeros((count, span), f32)
            total_in = jnp.zeros((count, span), f32)
            for s in range(experts):
                ref = ins[h * experts + s]
                total_out += columns[:, s : s + 1] * lax.dot_general(
                    picks[s], ref[0], CONTRACT_FIRST, preferred_element_type=f32
                )
                total_in += lax.dot_general(
                    picks[s], ref[1], CONTRACT_FIRST, preferred_element_type=f32
                )
            out[:, cols] = total_out.astype(bf16)
            d_in[:, cols] = total_in.astype(bf16)

    layer_out, d_tokens = call(
        collect, [shape(count, width)] * 2, [here, places, weights, *home]
    )

    d_tokens, arrived = lax.optimization_barrier((d_tokens, arrived))

    def finish(*refs):
        group = len(arrived[0])
        for i in range(PARTS):
            mine, *ins = refs[i * group : (i + 1) * group]
            cols = slice(i * strip, (i + 1) * strip)
            for m, out in enumerate(refs[PARTS * group :]):
                if two_hops:
                    from_first, from_second, last_second, last_first = ins
                    out[0, low, cols] = (
                        mine[m, low] + from_first[1, m].astype(f32) + last_second[m].astype(f32)
                    )
                    out[0, high, cols] = (
                        mine[m, high] + from_second[1, m].astype(f32) + last_first[m].astype(f32)
                    )
                else:
                    total = mine[m]
                    for ref in ins:
                        total = total + ref[m].astype(f32)
                    out[0, :, cols] = total

    grad_gate, grad_up, grad_down = call(
        finish, [shape(1, block, inner, dtype=f32)] * 3, sum(arrived, []), positions=False
    )
    return layer_out, d_tokens, grad_gate, grad_up, grad_down


def solution(mesh):
    by_token = P(("dp", "expert"), None)
    by_expert = P("expert", "dp", None)
    return jax.shard_map(
        shards,
        mesh=mesh,
        in_specs=(by_token,) * 3 + (by_expert,) * 3 + (by_token,),
        out_specs=(by_token,) * 2 + (by_expert,) * 3,
        check_vma=False,
    )
```

```python
import functools

import jax
import jax.numpy as jnp
from jax import lax
from jax.experimental import pallas as pl
from jax.experimental.pallas import tpu as pltpu
from jax.sharding import PartitionSpec as P

CAP = 32
CORES = 2
HALVES = 2
PARTS = 2
VMEM_BYTES = 48 * 1024 * 1024

CONTRACT_LAST = (((1,), (1,)), ((), ()))
CONTRACT_FIRST = (((0,), (0,)), ((), ()))


def call(kernel, out_shape, args, scratch=(), flops=0, positions=True):
    moved = sum(a.size * a.dtype.itemsize for a in args) + sum(
        o.size * o.dtype.itemsize for o in out_shape
    )
    return pl.pallas_call(
        kernel,
        out_shape=out_shape,
        in_specs=[
            pl.BlockSpec(memory_space=pltpu.SMEM if positions and i == 0 else pltpu.VMEM)
            for i in range(len(args))
        ],
        out_specs=[pl.BlockSpec(memory_space=pltpu.VMEM)] * len(out_shape),
        scratch_shapes=list(scratch),
        compiler_params=pltpu.CompilerParams(vmem_limit_bytes=VMEM_BYTES),
        cost_estimate=pl.CostEstimate(flops=flops, bytes_accessed=moved, transcendentals=0),
    )(*args)


def rank(hits):
    count = hits.shape[1]
    row = lax.broadcasted_iota(jnp.int32, (count, count), 0)
    column = lax.broadcasted_iota(jnp.int32, (count, count), 1)
    earlier = jnp.where(row < column, 1.0, 0.0).astype(jnp.bfloat16)
    return jnp.dot(hits.astype(jnp.bfloat16), earlier, preferred_element_type=jnp.float32)


def selector(place):
    slots = lax.broadcasted_iota(jnp.int32, (CAP, place.shape[1]), 0).astype(jnp.float32)
    return jnp.where(slots == place, 1.0, 0.0)


def shards(tokens, routes, gate_scale, w_gate, w_up, w_down, d_out):
    experts = lax.axis_size("expert")
    members = lax.axis_size("dp")
    chips = members // (HALVES * CORES)
    count, width = tokens.shape
    span = width // HALVES
    block, inner = w_gate.shape[1:]
    rows = experts * CAP
    bf16, f32 = jnp.bfloat16, jnp.float32
    spots = [(h, s) for h in range(HALVES) for s in range(experts)]

    member = lax.axis_index("dp")
    here = jnp.stack(
        [
            member // (chips * CORES),
            member // CORES % chips,
            member % CORES,
            lax.axis_index("expert"),
        ]
    ).astype(jnp.int32)

    def send(value, half=0, chip=0, core=0, shift=0):
        perm = []
        for d in range(members):
            to = d ^ (half * chips * CORES + chip * CORES + core)
            for e in range(experts):
                perm.append((d * experts + e, to * experts + (e + shift) % experts))
        return lax.ppermute(value, ("dp", "expert"), perm)

    def shape(*dims, dtype=bf16):
        return jax.ShapeDtypeStruct(dims, dtype)

    half_block = block // 2
    strip = inner // PARTS
    two_hops = chips == 4

    def pack(g_ref, u_ref, w_ref, *outs):
        for m, ref in enumerate((g_ref, u_ref, w_ref)):
            for k in range(2):
                for i, out in enumerate(outs):
                    out[k, m] = ref[
                        0, k * half_block : (k + 1) * half_block, i * strip : (i + 1) * strip
                    ]

    owns = list(
        pl.pallas_call(pack, out_shape=[shape(2, 3, half_block, strip)] * PARTS)(
            w_gate, w_up, w_down
        )
    )

    def first_hop(own):
        return [send(own, chip=o) for o in range(1, chips - 1 if two_hops else chips)]

    def second_hop(near):
        return [send(near[0][0], chip=2), send(near[1][1], chip=1)] if two_hops else []

    near = first_hop(owns[0])
    own_c = send(owns[0], core=1)

    def dispatch(at, r_ref, s_ref, t_ref, d_ref, *outs):
        *outs, p_ref, c_ref = outs
        route, scale = r_ref[...], s_ref[...]
        combine = scale / jnp.sum(scale, axis=0, keepdims=True)
        hits, weights = [], []
        for s in range(experts):
            match = route == lax.rem(at[3] + s, experts)
            hits.append(jnp.sum(jnp.where(match, 1.0, 0.0), axis=0, keepdims=True))
            weights.append(jnp.sum(jnp.where(match, combine, 0.0), axis=0, keepdims=True))
        pad = [jnp.zeros((8 - experts, count), f32)] if experts < 8 else []
        hits = jnp.concatenate(hits + pad, axis=0)
        places = jnp.where(hits > 0.0, rank(hits), -1.0)
        p_ref[...] = places
        c_ref[...] = jnp.concatenate(weights + pad, axis=0)
        for s in range(experts):
            pick = selector(places[s : s + 1])
            weight = jnp.sum(pick * weights[s], axis=1, keepdims=True)
            pick = pick.astype(bf16)
            for h in range(HALVES):
                side = jnp.bitwise_xor(at[0], h)
                cols = pl.ds(pl.multiple_of(side * span, span), span)
                out = outs[s].at[h]
                out[0] = jnp.dot(pick, t_ref[:, cols], preferred_element_type=f32).astype(bf16)
                out[1] = (
                    jnp.dot(pick, d_ref[:, cols], preferred_element_type=f32) * weight
                ).astype(bf16)

    *cut, places, weights = call(
        dispatch,
        [shape(HALVES, 2, CAP, span)] * experts + [shape(max(experts, 8), count, dtype=f32)] * 2,
        [here, routes.T, gate_scale.T, tokens, d_out],
    )
    *cut, own_c = lax.optimization_barrier((*cut, own_c))
    lead = [cut[0]] + [send(cut[s], shift=s) for s in range(1, experts)]
    follow = [send(m[1], half=1) for m in lead]
    pieces = [m[0] for m in lead] + follow

    *near, pieces[experts] = lax.optimization_barrier((*near, pieces[experts]))
    far = second_hop(near)
    reach = len(owns[:1]) + len(near) + len(far)
    parts = [[owns[0], *near, *far, own_c] + [send(m, core=1) for m in near + far]]
    for i in range(1, PARTS):
        owns[i], far = lax.optimization_barrier((owns[i], far or near[-1:]))
        near = first_hop(owns[i])
        far = second_hop(near)
        mine = [owns[i], *near, *far]
        parts.append(mine + [send(m, core=1) for m in mine])

    def assemble(at, refs, held, column):
        for i, ref in enumerate(refs):
            core, place = divmod(i, reach)
            for k in range(2):
                if len(ref.shape) == 4:
                    chip, part = place, ref.at[k]
                elif place - chips + 1 == k:
                    chip, part = chips - 1, ref
                else:
                    continue
                owner = jnp.bitwise_xor(at[1], chip) * CORES + jnp.bitwise_xor(at[2], core)
                start = pl.multiple_of(owner * block + k * half_block, half_block)
                for m in range(3):
                    held[m, pl.ds(start, half_block), column : column + strip] = part[m]

    def project(at, *refs):
        ins, refs = refs[: len(spots)], refs[len(spots) :]
        *ws, keep, give, held = refs
        assemble(at, ws, held, 0)
        for m, side in enumerate((0, 0, 1)):
            left = jnp.concatenate([ref[side] for ref in ins], axis=0)
            part = jnp.dot(left, held[m], preferred_element_type=f32)
            keep[m] = part
            give[m, :rows] = part[rows:].astype(bf16)
            give[m, rows:] = part[:rows].astype(bf16)

    keeps, gives = [], []
    for i in range(PARTS):
        keep, give = call(
            project,
            [shape(3, HALVES * rows, strip, dtype=f32), shape(3, HALVES * rows, strip)],
            [here, *pieces, *parts[i]],
            scratch=[pltpu.VMEM((3, span, strip), bf16)],
            flops=2 * 3 * HALVES * rows * span * strip,
        )
        keeps.append(keep)
        gives.append(give)
    cames = [send(gives[0], half=1)]

    def divide(at, *refs):
        ins, (stay, leave) = refs[: len(spots)], refs[len(spots) :]
        first = at[2] == 0
        for k in range(2):
            for i, ref in enumerate(ins):
                for chip in range(chips):
                    both = ref[k, :, chip * CORES * block : (chip + 1) * CORES * block]
                    low, high = both[:, :block], both[:, block:]
                    place = (k, slice(i * CAP, (i + 1) * CAP), slice(chip * block, (chip + 1) * block))
                    stay[place] = jnp.where(first, low, high)
                    leave[place] = jnp.where(first, high, low)

    keeps[0], apart = lax.optimization_barrier((keeps[0], tuple(pieces)))
    stay, leave = call(
        divide, [shape(2, HALVES * rows, chips * block)] * 2, [here, *apart]
    )
    across = send(leave, core=1)

    early = parts[-1][reach:-2]
    cames[0], across, early = lax.optimization_barrier((cames[0], across, early))
    parts[-1][reach:-2] = early
    for i in range(1, PARTS):
        cames.append(send(gives[i], half=1))

    def activate(at, keep_ref, came_ref, out):
        gate = keep_ref[0] + came_ref[0].astype(f32)
        up = keep_ref[1] + came_ref[1].astype(f32)
        d_hidden = keep_ref[2] + came_ref[2].astype(f32)
        sig = jax.nn.sigmoid(gate)
        act = gate * sig
        out[0] = (d_hidden * up * sig * (1.0 + gate * (1.0 - sig))).astype(bf16)
        out[1] = (d_hidden * act).astype(bf16)
        out[2] = (act * up).astype(bf16)

    low, high = slice(0, half_block), slice(half_block, block)

    def weigh(at, mine, theirs, x0, x1, *refs):
        outs, held = refs[:-1], refs[-1]
        for m in range(3):
            left = jnp.concatenate([x0[m // 2], x1[m // 2]], axis=0)
            right = jnp.concatenate([mine[m], theirs[m]], axis=0)
            held[...] = lax.dot_general(left, right, CONTRACT_FIRST, preferred_element_type=f32)

            def owned(o):
                start = pl.multiple_of(jnp.bitwise_xor(at[1], o) * block, block)
                return held[pl.ds(start, block), :]

            outs[0][m] = owned(0)
            if two_hops:
                _, by_first, by_second, kept = outs
                first, second, across_it = owned(1), owned(2), owned(3)
                by_first[0, m] = across_it[low].astype(bf16)
                by_first[1, m] = first[low].astype(bf16)
                by_second[0, m] = across_it[high].astype(bf16)
                by_second[1, m] = second[high].astype(bf16)
                kept[0, m] = second[low]
                kept[1, m] = first[high]
            else:
                for o in range(1, chips):
                    outs[o][m] = owned(o).astype(bf16)

    def weigh_with(mine, theirs):
        if two_hops:
            others = [shape(2, 3, half_block, strip)] * 2
            others.append(shape(2, 3, half_block, strip, dtype=f32))
        else:
            others = [shape(3, block, strip)] * (chips - 1)
        return list(
            call(
                weigh,
                [shape(3, block, strip, dtype=f32), *others],
                [here, mine, theirs, stay, across],
                scratch=[pltpu.VMEM((chips * block, strip), f32)],
                flops=2 * 3 * CORES * HALVES * rows * chips * block * strip,
            )
        )

    def relay(kept, from_first, from_second, to_second, to_first):
        to_second[...] = (kept[0] + from_first[0].astype(f32)).astype(bf16)
        to_first[...] = (kept[1] + from_second[0].astype(f32)).astype(bf16)

    def leave_first(grads):
        if two_hops:
            return [send(grads[1], chip=1), send(grads[2], chip=2)]
        return [send(grads[o], chip=o) for o in range(1, chips)]

    def join(grads, came):
        if not two_hops:
            return []
        return list(
            call(relay, [shape(3, half_block, strip)] * 2, [grads[3], *came], positions=False)
        )

    def leave_second(joined):
        return [send(m, chip=2 - i) for i, m in enumerate(joined)]

    inside, inside_c, arrived = [], [], []
    for i in range(PARTS):
        inside += call(
            activate, [shape(3, HALVES * rows, strip)], [here, keeps[i], cames[i]]
        )
        inside_c.append(send(inside[i], core=1))
        if i + 1 < PARTS:
            grads = weigh_with(inside[i], inside_c[i])
            grads[0], cames[i + 1] = lax.optimization_barrier((grads[0], cames[i + 1]))
            hop = leave_first(grads)
            hop[0], cames[i + 1] = lax.optimization_barrier((hop[0], cames[i + 1]))
            joined = join(grads, hop)
            arrived.append([grads[0], *hop, *leave_second(joined)])

    def expand(at, *refs):
        count_outs = HALVES * experts + 1
        ins, ws, (*outs, held) = refs[:PARTS], refs[PARTS:-count_outs], refs[-count_outs:]
        for i in range(PARTS):
            assemble(at, ws[i * len(parts[0]) : (i + 1) * len(parts[0])], held, i * strip)
        left = [jnp.concatenate([ref[m] for ref in ins], axis=1) for m in range(3)]
        out = lax.dot_general(left[2], held[2], CONTRACT_LAST, preferred_element_type=f32)
        d_in = lax.dot_general(
            left[0], held[0], CONTRACT_LAST, preferred_element_type=f32
        ) + lax.dot_general(left[1], held[1], CONTRACT_LAST, preferred_element_type=f32)
        for s in range(experts):
            for h in range(HALVES):
                part = slice((h * experts + s) * CAP, (h * experts + s + 1) * CAP)
                ref = outs[h * experts + s]
                ref[0] = out[part].astype(bf16)
                ref[1] = d_in[part].astype(bf16)

    back = call(
        expand,
        [shape(2, CAP, span)] * len(spots),
        [here, *inside, *sum(parts, [])],
        scratch=[pltpu.VMEM((3, span, inner), bf16)],
        flops=2 * 3 * HALVES * rows * span * inner,
    )
    *back, inside_c[-1] = lax.optimization_barrier((*back, inside_c[-1]))
    last = weigh_with(inside[-1], inside_c[-1])
    hop = leave_first(last)
    joined = join(last, hop)
    home = {(0, 0): back[0]}
    for i, (h, s) in enumerate(spots):
        if h > 0:
            home[h, s] = send(back[i], half=h, shift=-s)
    hop[0], near_back = lax.optimization_barrier((hop[0], tuple(back[1:experts])))
    for s in range(1, experts):
        home[0, s] = send(near_back[s - 1], shift=-s)
    home = [home[spot] for spot in spots]
    arrived.append([last[0], *hop, *leave_second(joined)])

    def collect(at, p_ref, w_ref, *refs):
        ins, (out, d_in) = refs[: len(spots)], refs[len(spots) :]
        picks, coarse, fine = [], [], []
        for s in range(experts):
            pick = selector(p_ref[s : s + 1])
            heavy = pick * w_ref[s : s + 1]
            picks.append(pick.astype(bf16))
            coarse.append(heavy.astype(bf16))
            fine.append((heavy - coarse[s].astype(f32)).astype(bf16))
        picks = jnp.concatenate(picks, axis=0)
        scaled = jnp.concatenate(coarse + fine, axis=0)
        for h in range(HALVES):
            side = jnp.bitwise_xor(at[0], h)
            cols = pl.ds(pl.multiple_of(side * span, span), span)
            part = ins[h * experts : (h + 1) * experts]
            rows_out = jnp.concatenate([ref[0] for ref in part] * 2, axis=0)
            rows_in = jnp.concatenate([ref[1] for ref in part], axis=0)
            out[:, cols] = lax.dot_general(
                scaled, rows_out, CONTRACT_FIRST, preferred_element_type=f32
            ).astype(bf16)
            d_in[:, cols] = lax.dot_general(
                picks, rows_in, CONTRACT_FIRST, preferred_element_type=f32
            ).astype(bf16)

    layer_out, d_tokens = call(
        collect, [shape(count, width)] * 2, [here, places, weights, *home]
    )

    d_tokens, arrived = lax.optimization_barrier((d_tokens, arrived))

    def finish(*refs):
        group = len(arrived[0])
        for i in range(PARTS):
            mine, *ins = refs[i * group : (i + 1) * group]
            cols = slice(i * strip, (i + 1) * strip)
            for m, out in enumerate(refs[PARTS * group :]):
                if two_hops:
                    from_first, from_second, last_second, last_first = ins
                    out[0, low, cols] = (
                        mine[m, low] + from_first[1, m].astype(f32) + last_second[m].astype(f32)
                    )
                    out[0, high, cols] = (
                        mine[m, high] + from_second[1, m].astype(f32) + last_first[m].astype(f32)
                    )
                else:
                    total = mine[m]
                    for ref in ins:
                        total = total + ref[m].astype(f32)
                    out[0, :, cols] = total

    grad_gate, grad_up, grad_down = call(
        finish, [shape(1, block, inner, dtype=f32)] * 3, sum(arrived, []), positions=False
    )
    return layer_out, d_tokens, grad_gate, grad_up, grad_down


def solution(mesh):
    by_token = P(("dp", "expert"), None)
    by_expert = P("expert", "dp", None)
    return jax.shard_map(
        shards,
        mesh=mesh,
        in_specs=(by_token,) * 3 + (by_expert,) * 3 + (by_token,),
        out_specs=(by_token,) * 2 + (by_expert,) * 3,
        check_vma=False,
    )
```
